32 devices in a mesh: sub: 8 (over z, x), grp: 4 (over y, core).
Axes of the slice: x: 2, y: 2, z: 4, core: 2. Of those that a mesh axis runs over, the one named last changes fastest.
Arguments:
- loads: float32 [4, 16, 2, 48, 256], P('grp', 'sub'), may hold values from -18 to 18
- inv_schur: bfloat16 [4, 16, 1024, 1024], P('grp', 'sub'), as said below
- schur: bfloat16 [4, 16, 1024, 1024], P('grp', 'sub'), as said below
- coarse_map: bfloat16 [4, 16, 12, 1024], P('grp', 'sub'), may hold values from -0.75 to 0.75
- coarse_inverse: float32 [4, 16, 12, 4, 192], P('grp', 'sub'), as said below
- face_rows: int32 [4, 16, 1024], P('grp', 'sub'), may hold values from 0 to 1023, each once within a row
- face_len: int32 [4, 16, 2], P('grp', 'sub'), may hold values from 64 to 256
Outputs:
- multipliers: float32 [4, 16, 2, 48, 256], P('grp', 'sub')
- residual: float32 [4, 16, 2, 48, 256], P('grp', 'sub')
The draws below stay inside these ranges and needn't reach their ends.
Inputs may be any that keep to these rules, and one draw needn't show every extreme that they name: `inv_schur`: each subdomain's matrix is symmetric and positive definite. `schur`: each subdomain's matrix is symmetric and positive definite. `coarse_inverse`: seen as a [768, 768] matrix it is symmetric and positive definite. `face_rows`: each subdomain's row is a permutation of 0 to 1023.
All inputs are finite; a program needn't handle non-finite values.
Results may differ from the reference program's by a relative error of at most 0.025.
Values sent between devices are 32-bit elements; how exact they have to be, the bound alone decides.
A program may use at most 128 MiB of HBM per device.

```python
import math
import jax
import jax.numpy as jnp
from jax import lax

ORDER = 1024
FACE = 256
LOADS = 48
CDOF = 12
ITERS = 3
SPAN = 16
CYCLE = 4
NCOARSE = 768


def symmetric_block(key, blocks, extent, spread):
    random_part = jax.random.normal(key, (blocks, extent, extent), jnp.float32)
    random_part = random_part * (spread / math.sqrt(extent))
    paired = (random_part + jnp.swapaxes(random_part, 1, 2)) * 0.7071
    return paired + jnp.eye(extent, dtype=jnp.float32)[None]


def draw_inv_schur(key, part):
    block = symmetric_block(jax.random.fold_in(key, 11), CYCLE * SPAN, ORDER, 0.45)
    return block.reshape(CYCLE, SPAN, ORDER, ORDER).astype(jnp.bfloat16)


def draw_schur(key, part):
    block = symmetric_block(jax.random.fold_in(key, 23), CYCLE * SPAN, ORDER, 0.45)
    return block.reshape(CYCLE, SPAN, ORDER, ORDER).astype(jnp.bfloat16)


def draw_coarse_inverse(key, part):
    block = symmetric_block(jax.random.fold_in(key, 37), 1, NCOARSE, 0.4)
    return block[0].reshape(CYCLE, SPAN, CDOF, CYCLE, SPAN * CDOF)


def draw_loads(key, part):
    first, second, third = jax.random.split(jax.random.fold_in(key, 41), 3)
    shape_all = (CYCLE, SPAN, 2, LOADS, FACE)
    case_scale = 10.0 ** jax.random.uniform(second, (1, 1, 1, LOADS, 1), jnp.float32)
    entry_scale = 10.0 ** jax.random.uniform(third, (CYCLE, SPAN, 2, 1, FACE), jnp.float32)
    ramp = 3.0 ** (jnp.arange(SPAN, dtype=jnp.float32) / max(SPAN - 1, 1))
    ramp = ramp.reshape(1, SPAN, 1, 1, 1)
    base = jnp.clip(jax.random.normal(first, shape_all, jnp.float32), -6.0, 6.0)
    return jnp.clip(0.1 * base * case_scale * entry_scale * ramp, -18.0, 18.0)


def draw_face_len(key, part):
    first, second, third = jax.random.split(jax.random.fold_in(key, 53), 3)
    total = CYCLE * SPAN * 2
    lengths = jax.random.randint(first, (CYCLE, SPAN, 2), FACE // 4, FACE + 1)
    flat_index = jnp.arange(total).reshape(CYCLE, SPAN, 2)
    top_spot = jax.random.randint(second, (), 0, total)
    low_spot = (top_spot + 1 + jax.random.randint(third, (), 0, total - 1)) % total
    lengths = jnp.where(flat_index == top_spot, FACE, lengths)
    lengths = jnp.where(flat_index == low_spot, FACE // 4, lengths)
    return lengths.astype(jnp.int32)


def block_scale(stream_key, shape, cuts, smallest, top_value):
    level = 1.0
    for dim, parts in cuts:
        steps = jax.random.uniform(jax.random.fold_in(jax.random.fold_in(stream_key, 6), dim), (parts,), jnp.float32, smallest / len(cuts), top_value / len(cuts))
        level = level * jnp.repeat(jnp.exp(steps), shape[dim] // parts).reshape((-1,) + (1,) * (len(shape) - 1 - dim))
    return level


def gaussian(own_key, shape, scale, most, cuts=(), kind=jnp.bfloat16):
    array = jax.random.normal(own_key, shape, jnp.float32) * scale
    if len(cuts) > 0:
        array = block_scale(own_key, shape, cuts, -0.22, 0.18) * array
    return jnp.clip(array, min=-most, max=most).astype(kind)


def setup_inputs(seed: int = 0) -> dict:
    splits = jax.random.split(jax.random.key(seed), 8)
    return {
        "loads": draw_loads(jax.random.fold_in(splits[7], 71), 0),
        "inv_schur": draw_inv_schur(jax.random.fold_in(splits[7], 71), 0),
        "schur": draw_schur(jax.random.fold_in(splits[7], 71), 0),
        "coarse_map": gaussian(splits[3], (CYCLE, SPAN, CDOF, ORDER), (4 * ORDER ** -0.5), 0.75, ((0, 4), (1, 8))),
        "coarse_inverse": draw_coarse_inverse(jax.random.fold_in(splits[7], 71), 0),
        "face_rows": jax.vmap(lambda own: jax.random.permutation(own, ORDER))(jax.random.split(splits[5], CYCLE * SPAN)).reshape((CYCLE, SPAN, ORDER)).astype(jnp.int32),
        "face_len": draw_face_len(jax.random.fold_in(splits[7], 71), 0),
    }


def face_live(face_len):
    positions = jnp.arange(FACE)
    columns = jnp.arange(SPAN)
    along = (positions[None, None, :] < face_len[:, :, 0:1]) & (columns[None, :, None] < SPAN - 1)
    beside_all = positions[None, None, :] < face_len[:, :, 1:2]
    return jnp.stack([along, beside_all], axis=2).astype(jnp.float32)[:, :, :, None, :]

def spread_faces(faces):
    along = faces[:, :, 0]
    beside_all = faces[:, :, 1]
    from_left = jnp.concatenate([jnp.zeros_like(along[:, :1]), along[:, :-1]], axis=1)
    from_below = jnp.roll(beside_all, 1, axis=0)
    stacked = jnp.stack([-from_left, along, -from_below, beside_all], axis=3)
    return stacked.reshape(CYCLE * SPAN, LOADS, ORDER)

def collect_jumps(field, live):
    pieces = field.reshape(CYCLE, SPAN, LOADS, 4, FACE)
    from_right = jnp.concatenate([pieces[:, 1:, :, 0], jnp.zeros_like(pieces[:, :1, :, 0])], axis=1)
    from_above = jnp.roll(pieces[:, :, :, 2], -1, axis=0)
    jumps = jnp.stack([pieces[:, :, :, 1] - from_right, pieces[:, :, :, 3] - from_above], axis=2)
    return jumps * live

def place_rows(slotted, slot_rows):
    empty = jnp.zeros((LOADS, ORDER), jnp.bfloat16)
    return empty.at[:, slot_rows].set(slotted.astype(jnp.bfloat16))

def apply_operator(direction, live, inv_flat, basis_flat, rows_flat, coarse_matrix):
    slotted = spread_faces(direction)

    def local_solve(item):
        piece_slots, slot_rows, matrix, basis_rows = item
        placed = place_rows(piece_slots, slot_rows)
        local_part = jnp.dot(placed.astype(jnp.float32), matrix.astype(jnp.float32), preferred_element_type=jnp.float32)[:, slot_rows]
        terms = jnp.dot(placed.astype(jnp.float32), basis_rows.T.astype(jnp.float32), preferred_element_type=jnp.float32)
        return (local_part, terms)
    local_part, terms = lax.map(local_solve, (slotted, rows_flat, inv_flat, basis_flat))
    flat_terms = jnp.transpose(terms, (1, 0, 2)).reshape(LOADS, NCOARSE)
    solved = jnp.dot(flat_terms, coarse_matrix.T, precision=lax.Precision.HIGHEST)
    corrections = jnp.transpose(solved.reshape(LOADS, CYCLE * SPAN, CDOF), (1, 0, 2)).astype(jnp.bfloat16)

    def add_coarse(item):
        correction, slot_rows, basis_rows = item
        return jnp.dot(correction.astype(jnp.float32), basis_rows.astype(jnp.float32), preferred_element_type=jnp.float32)[:, slot_rows]
    response = local_part + lax.map(add_coarse, (corrections, rows_flat, basis_flat))
    return collect_jumps(response, live)

def apply_precond(resid, live, schur_flat, rows_flat):
    slotted = spread_faces(resid)

    def local_smooth(item):
        piece_slots, slot_rows, matrix = item
        placed = place_rows(piece_slots, slot_rows)
        return jnp.dot(placed.astype(jnp.float32), matrix.astype(jnp.float32), preferred_element_type=jnp.float32)[:, slot_rows]
    smoothed = lax.map(local_smooth, (slotted, rows_flat, schur_flat))
    return collect_jumps(smoothed, live)

def inner_gram(first, second):
    return jnp.einsum('gjsat,gjsbt->ab', first, second, precision=lax.Precision.HIGHEST)

def combine(weights, faces):
    return jnp.einsum('ab,gjsat->gjsbt', weights, faces, precision=lax.Precision.HIGHEST)

def gram_solve(matrix, right):
    return jax.scipy.linalg.cho_solve((jnp.linalg.cholesky(matrix), True), right)

def reference(loads, inv_schur, schur, coarse_map, coarse_inverse, face_rows, face_len):
    live = face_live(face_len)
    rows_flat = face_rows.reshape(CYCLE * SPAN, ORDER)
    inv_flat = inv_schur.reshape(CYCLE * SPAN, ORDER, ORDER)
    schur_flat = schur.reshape(CYCLE * SPAN, ORDER, ORDER)
    basis_flat = coarse_map.reshape(CYCLE * SPAN, CDOF, ORDER)
    coarse_matrix = coarse_inverse.reshape(NCOARSE, NCOARSE)
    residual = loads * live
    multipliers = jnp.zeros_like(residual)
    search = apply_precond(residual, live, schur_flat, rows_flat)
    precond_gram = inner_gram(search, residual)
    direction = search
    for iteration in range(ITERS):
        image_faces = apply_operator(direction, live, inv_flat, basis_flat, rows_flat, coarse_matrix)
        curvature = inner_gram(direction, image_faces)
        step_size = gram_solve(curvature, precond_gram)
        multipliers = multipliers + combine(step_size, direction)
        residual = residual - combine(step_size, image_faces)
        if iteration + 1 < ITERS:
            search = apply_precond(residual, live, schur_flat, rows_flat)
            new_gram = inner_gram(search, residual)
            conjugate = gram_solve(precond_gram, new_gram)
            direction = search + combine(conjugate, direction)
            precond_gram = new_gram
    return (multipliers, residual)
```

```python
import functools

import jax
import jax.numpy as jnp
from jax import lax
from jax.experimental import pallas as pl
from jax.experimental.pallas import tpu as pltpu
from jax.sharding import PartitionSpec as P

FACE = 256
LOADS = 48
CDOF = 12
ITERS = 3
ORDER = 1024
PADQ = 16
HALF = 64
LANES = 128
HIGHEST = lax.Precision.HIGHEST
MESH = pl.DeviceIdType.MESH
F32 = jnp.float32
BF16 = jnp.bfloat16


def dot_nn(a, b, precision=None):
    return lax.dot_general(
        a, b, (((1,), (0,)), ((), ())), precision=precision, preferred_element_type=F32
    )


def dot_nt(a, b, precision=None):
    return lax.dot_general(
        a, b, (((1,), (1,)), ((), ())), precision=precision, preferred_element_type=F32
    )


def widen(block):
    rows, columns = block.shape
    return jnp.concatenate([block, jnp.zeros((rows, LANES - columns), F32)], axis=1)


def pack_gram(gram):
    wide = widen(gram)
    half = LOADS // 2
    return wide[:half] + pltpu.roll(wide[half:], HALF, 1)


def unpack_gram(packed):
    return jnp.concatenate([packed, pltpu.roll(packed, HALF, 1)], axis=0)


def transposed(wide):
    return widen(jnp.transpose(wide)[:LOADS])


def eliminate(matrix, right):
    lane = lax.broadcasted_iota(jnp.int32, (LOADS, LANES), 1)
    row = lax.broadcasted_iota(jnp.int32, (LOADS, LANES), 0)
    symmetric = 0.5 * (matrix + transposed(matrix))
    both = jnp.where(lane < HALF, symmetric, pltpu.roll(right, HALF, 1))
    for k in range(LOADS):
        pivot_row = both[k : k + 1, :]
        scaled = pivot_row * (1.0 / both[k : k + 1, k : k + 1])
        both = jnp.where(row == k, scaled, both - both[:, k : k + 1] * scaled)
    return pltpu.roll(both, HALF, 1)


def kernel(
    n, ng,
    loads, inv_hbm, schur_hbm, cmap, cinv, frow, flen,
    mult_out, res_out,
    amat, qmat, tmat, pt, pcol, basis, field, from_left, from_right, from_above, from_below,
    live, resid, direc, gram_g, gram_s, term_g, part_s, part_r, cin_g, cin_t,
    load_sem, halo_ss, halo_rs, live_ss, live_rs, cin_ss, cin_rs,
    gg_ss, gg_rs, gs_ss, gs_rs, tg_ss, tg_rs, ps_ss, ps_rs,
):
    s = lax.axis_index("sub")
    g = lax.axis_index("grp")
    right, left = lax.rem(s + 1, n), lax.rem(s + n - 1, n)
    above, below = lax.rem(g + 1, ng), lax.rem(g + ng - 1, ng)

    loaded = []
    for index in range(4):
        source = (schur_hbm if index < 2 else inv_hbm).at[index % 2]
        loaded.append(pltpu.make_async_copy(source, amat.at[index], load_sem.at[index]))
        loaded[-1].start()

    barrier = pltpu.get_barrier_semaphore()
    for i in range(1, ng):
        pl.semaphore_signal(
            barrier, inc=1, device_id={"grp": lax.rem(g + i, ng)}, device_id_type=MESH
        )

    def greet(i, carry):
        pl.semaphore_signal(
            barrier, inc=1, device_id={"sub": lax.rem(s + i, n)}, device_id_type=MESH
        )
        return carry

    lax.fori_loop(1, n, greet, 0)

    position = lax.broadcasted_iota(jnp.int32, (8, FACE), 1)
    for k in range(2):
        along = (position < flen[k, 0]) & (2 * s + k < 2 * n - 1)
        around = position < flen[k, 1]
        live[1, k] = jnp.where(along, 1.0, 0.0)
        live[3, k] = jnp.where(around, 1.0, 0.0)
        field[0, 0, k] = jnp.zeros((LOADS, FACE), F32)
        field[0, 2, k] = jnp.zeros((LOADS, FACE), F32)
        field[0, 1, k] = loads[k, 0]
        field[0, 3, k] = loads[k, 1]
    live[0, 1] = live[1, 0]
    cin_g[pl.ds(g, 1)] = cinv[pl.ds(g, 1)]

    sends = []

    def send(src, dst, send_sem, recv_sem, to):
        copy = pltpu.make_async_remote_copy(
            src_ref=src, dst_ref=dst, send_sem=send_sem, recv_sem=recv_sem,
            device_id=to, device_id_type=MESH,
        )
        copy.start()
        sends.append(copy)
        return copy

    def halo_start(r, first=False):
        copies = [
            send(field.at[r, 1, 1], from_left.at[r], halo_ss.at[r, 0], halo_rs.at[r, 0], {"sub": right}),
            send(field.at[r, 3], from_below.at[r], halo_ss.at[r, 1], halo_rs.at[r, 1], {"grp": above}),
        ]
        if not first:
            copies += [
                send(field.at[r, 0, 0], from_right.at[r], halo_ss.at[r, 2], halo_rs.at[r, 2], {"sub": left}),
                send(field.at[r, 2], from_above.at[r], halo_ss.at[r, 3], halo_rs.at[r, 3], {"grp": below}),
            ]
        return copies

    def jumps(r, copies):
        for copy in copies:
            copy.wait_recv()
        first = len(copies) == 2
        pieces = []
        for k in range(2):
            for slot in range(4):
                if slot == 0:
                    other = from_left[r] if k == 0 else field[r, 1, 0]
                elif slot == 1:
                    other = field[r, 0, 1] if k == 0 else (None if first else from_right[r])
                elif slot == 2:
                    other = from_below[r, k]
                else:
                    other = None if first else from_above[r, k]
                mine = field[r, slot, k]
                jump = mine if other is None else mine - other
                pieces.append(jnp.where(live[slot, k, 0:1, :] > 0.5, jump, 0.0))
        return jnp.concatenate(pieces, axis=1)

    def store_field(r, values):
        for k in range(2):
            for slot in range(4):
                field[r, slot, k] = values[k][:, slot * FACE : (slot + 1) * FACE]

    def group_start(buffer, r, ss, rs):
        for i in range(1, ng):
            pltpu.make_async_remote_copy(
                src_ref=buffer.at[r, g], dst_ref=buffer.at[r, g],
                send_sem=ss.at[r], recv_sem=rs.at[r],
                device_id={"grp": lax.rem(g + i, ng)}, device_id_type=MESH,
            ).start()
        whole = pltpu.make_async_remote_copy(
            src_ref=buffer.at[r, pl.ds(0, ng - 1)], dst_ref=buffer.at[r, pl.ds(0, ng - 1)],
            send_sem=ss.at[r], recv_sem=rs.at[r],
            device_id={"grp": above}, device_id_type=MESH,
        )
        sends.append(whole)
        return whole

    def span_start(source, buffer, r, ss, rs, scatter):
        def step(i, carry):
            peer = lax.rem(s + i, n)
            pltpu.make_async_remote_copy(
                src_ref=source.at[r, peer if scatter else s], dst_ref=buffer.at[r, s],
                send_sem=ss.at[r], recv_sem=rs.at[r],
                device_id={"sub": peer}, device_id_type=MESH,
            ).start()
            return carry

        lax.fori_loop(1, n, step, 0)
        whole = pltpu.make_async_remote_copy(
            src_ref=buffer.at[r, pl.ds(0, n - 1)], dst_ref=buffer.at[r, pl.ds(0, n - 1)],
            send_sem=ss.at[r], recv_sem=rs.at[r],
            device_id={"sub": right}, device_id_type=MESH,
        )
        sends.append(whole)
        return whole

    def reduce_start(r, gram):
        gram_g[r, g] = pack_gram(gram)
        return group_start(gram_g, r, gg_ss, gg_rs)

    def reduce_middle(r, whole):
        whole.wait_recv()
        gram_s[r, s] = jnp.sum(gram_g[r], axis=0)
        return span_start(gram_s, gram_s, r, gs_ss, gs_rs, False)

    def reduce_end(r, whole):
        whole.wait_recv()
        return unpack_gram(jnp.sum(gram_s[r], axis=0))

    pl.semaphore_wait(barrier, ng - 1 + n - 1)

    halo = halo_start(0, first=True)
    live_copies = [
        send(live.at[1, 1], live.at[0, 0], live_ss.at[0], live_rs.at[0], {"sub": right}),
        send(live.at[3], live.at[2], live_ss.at[1], live_rs.at[1], {"grp": above}),
    ]
    cin_copies = []
    for i in range(1, ng):
        peer = lax.rem(g + i, ng)
        cin_copies.append(
            send(cinv.at[peer], cin_g.at[g], cin_ss.at[i], cin_rs.at[i], {"grp": peer})
        )

    for k in range(2):
        rows = frow[k : k + 1, :]
        pcol[k] = jnp.transpose(jnp.broadcast_to(rows, (LANES, ORDER)))

        @pl.loop(0, ORDER // FACE)
        def _(i, k=k):
            at = pl.multiple_of(i * FACE, FACE)
            index = lax.broadcasted_iota(jnp.int32, (FACE, ORDER), 0) + at
            pt[k, pl.ds(at, FACE)] = jnp.where(index == frow[k : k + 1, :], 1.0, 0.0).astype(BF16)

    def reorder(index):
        k = index % 2
        loaded[index].wait()

        @pl.loop(0, ORDER // FACE)
        def _(i):
            at = pl.multiple_of(i * FACE, FACE)
            tmat[pl.ds(at, FACE)] = dot_nn(amat[index, pl.ds(at, FACE)], pt[k]).astype(BF16)

        @pl.loop(0, ORDER // FACE)
        def _(i):
            at = pl.multiple_of(i * FACE, FACE)
            block = pcol[k, pl.ds(at, FACE)]
            wide = jnp.concatenate([block] * (ORDER // LANES), axis=1)
            index_of = lax.broadcasted_iota(jnp.int32, (FACE, ORDER), 1)
            pick = jnp.where(index_of == wide, 1.0, 0.0).astype(BF16)
            qmat[index, pl.ds(at, FACE)] = dot_nn(pick, tmat[...]).astype(BF16)

    def apply(base, rounded):
        return [
            dot_nn(rounded[:, k * ORDER : (k + 1) * ORDER], qmat[base + k]) for k in range(2)
        ]

    reorder(0)
    reorder(1)
    for copy in live_copies:
        copy.wait_recv()
    resid[...] = jumps(0, halo)

    def precondition(r, count):
        values = apply(0, resid[...].astype(BF16))
        store_field(r, values)
        halo = halo_start(r)
        gram = dot_nt(jnp.concatenate(values, axis=1), resid[...], HIGHEST)
        return halo, reduce_start(count, gram)

    halo, stage = precondition(1, 0)
    for k in range(2):
        basis[k] = dot_nn(cmap[k], pt[k]).astype(BF16)
    reorder(2)
    stage = reduce_middle(0, stage)
    for copy in cin_copies:
        copy.wait_recv()
    wide = jnp.concatenate(
        [cin_g[group, k] for k in range(2) for group in range(ng)], axis=0
    )
    cin_t[...] = jnp.transpose(wide)
    reorder(3)
    direc[...] = jumps(1, halo)
    precond_gram = reduce_end(0, stage)

    lane = lax.broadcasted_iota(jnp.int32, (LOADS, LANES), 1)
    row = lax.broadcasted_iota(jnp.int32, (LOADS, LANES), 0)
    identity = jnp.where(lane == row, 1.0, 0.0)

    r, count = 2, 1
    for iteration in range(ITERS):
        rounded = direc[...].astype(BF16)
        terms = [
            widen(dot_nt(basis[k], rounded[:, k * ORDER : (k + 1) * ORDER])) for k in range(2)
        ]
        term_g[iteration, g] = terms[0] + pltpu.roll(terms[1], HALF, 1)
        stage = group_start(term_g, iteration, tg_ss, tg_rs)
        values = apply(2, rounded)
        stage.wait_recv()
        gathered = term_g[iteration].reshape(ng * PADQ, LANES)
        stacked = jnp.concatenate([gathered, pltpu.roll(gathered, HALF, 1)], axis=0)
        shares = dot_nn(cin_t[...], stacked, HIGHEST)
        low = lax.broadcasted_iota(jnp.int32, (n * PADQ, LANES), 1) < HALF
        shares = jnp.where(low, shares[: n * PADQ], pltpu.roll(shares[n * PADQ :], HALF, 1))
        part_s[iteration] = shares.reshape(n, PADQ, LANES)
        part_r[iteration, pl.ds(s, 1)] = part_s[iteration, pl.ds(s, 1)]
        stage = span_start(part_s, part_r, iteration, ps_ss, ps_rs, True)
        stage.wait_recv()
        solved = jnp.transpose(jnp.sum(part_r[iteration], axis=0)).astype(BF16)
        values = [
            values[k] + dot_nn(solved[k * HALF : k * HALF + LOADS], basis[k]) for k in range(2)
        ]
        store_field(r, values)
        halo = halo_start(r)
        gram = dot_nt(direc[...], jnp.concatenate(values, axis=1), HIGHEST)
        stage = reduce_start(count, gram)
        stage = reduce_middle(count, stage)
        image = jumps(r, halo)
        curvature = reduce_end(count, stage)
        r, count = r + 1, count + 1
        step_size = jnp.transpose(eliminate(curvature, precond_gram))[:LOADS]
        resid[...] -= dot_nn(step_size, image, HIGHEST)
        more = iteration + 1 < ITERS
        if more:
            halo, stage = precondition(r, count)
        for k in range(2):
            for side in range(2):
                at = k * ORDER + (2 * side + 1) * FACE
                part = dot_nn(step_size, direc[:, at : at + FACE], HIGHEST)
                if iteration > 0:
                    part = mult_out[k, side] + part
                mult_out[k, side] = part
        if more:
            stage = reduce_middle(count, stage)
            inverse = eliminate(precond_gram, identity)
            search = jumps(r, halo)
            new_gram = reduce_end(count, stage)
            conjugate = dot_nn(inverse[:, :LOADS], new_gram, HIGHEST)
            weights = jnp.transpose(conjugate)[:LOADS]
            direc[...] = search + dot_nn(weights, direc[...], HIGHEST)
            precond_gram = new_gram
            r, count = r + 1, count + 1

    for k in range(2):
        for side in range(2):
            at = k * ORDER + (2 * side + 1) * FACE
            res_out[k, side] = resid[:, at : at + FACE]
    for copy in sends:
        copy.wait_send()


def body(n, ng, loads, inv_schur, schur, coarse_map, coarse_inverse, face_rows, face_len):
    basis_rows = jnp.pad(coarse_map[0], ((0, 0), (0, PADQ - CDOF), (0, 0)))
    own = coarse_inverse[0].reshape(2, CDOF, ng, n, 2, CDOF)
    own = jnp.transpose(own, (2, 0, 1, 4, 3, 5))
    pad = PADQ - CDOF
    own = jnp.pad(own, ((0, 0), (0, 0), (0, pad), (0, 0), (0, 0), (0, pad)))
    own = own.reshape(ng, 2, PADQ, 2 * n * PADQ)

    rounds, grams = 2 * ITERS + 1, 2 * ITERS
    vmem, dma = pltpu.VMEM, pltpu.SemaphoreType.DMA
    faces = jax.ShapeDtypeStruct((2, 2, LOADS, FACE), F32)
    in_vmem = pl.BlockSpec(memory_space=pltpu.VMEM)
    in_hbm = pl.BlockSpec(memory_space=pl.ANY)
    multipliers, residual = pl.pallas_call(
        functools.partial(kernel, n, ng),
        out_shape=(faces, faces),
        in_specs=[
            in_vmem, in_hbm, in_hbm, in_vmem, in_vmem, in_vmem,
            pl.BlockSpec(memory_space=pltpu.SMEM),
        ],
        out_specs=(in_vmem, in_vmem),
        scratch_shapes=[
            vmem((4, ORDER, ORDER), BF16),
            vmem((4, ORDER, ORDER), BF16),
            vmem((ORDER, ORDER), BF16),
            vmem((2, ORDER, ORDER), BF16),
            vmem((2, ORDER, LANES), jnp.int32),
            vmem((2, PADQ, ORDER), BF16),
            vmem((rounds, 4, 2, LOADS, FACE), F32),
            vmem((rounds, LOADS, FACE), F32),
            vmem((rounds, LOADS, FACE), F32),
            vmem((rounds, 2, LOADS, FACE), F32),
            vmem((rounds, 2, LOADS, FACE), F32),
            vmem((4, 2, 8, FACE), F32),
            vmem((LOADS, 2 * ORDER), F32),
            vmem((LOADS, 2 * ORDER), F32),
            vmem((grams, ng, LOADS // 2, LANES), F32),
            vmem((grams, n, LOADS // 2, LANES), F32),
            vmem((ITERS, ng, PADQ, LANES), F32),
            vmem((ITERS, n, PADQ, LANES), F32),
            vmem((ITERS, n, PADQ, LANES), F32),
            vmem((ng, 2, PADQ, 2 * n * PADQ), F32),
            vmem((2 * n * PADQ, 2 * ng * PADQ), F32),
            dma((4,)),
            dma((rounds, 4)), dma((rounds, 4)),
            dma((2,)), dma((2,)),
            dma((ng,)), dma((ng,)),
            dma((grams,)), dma((grams,)),
            dma((grams,)), dma((grams,)),
            dma((ITERS,)), dma((ITERS,)),
            dma((ITERS,)), dma((ITERS,)),
        ],
        compiler_params=pltpu.CompilerParams(
            collective_id=0, has_side_effects=True, vmem_limit_bytes=56 * 1024 * 1024
        ),
    )(loads[0], inv_schur[0], schur[0], basis_rows, own, face_rows[0], face_len[0])
    return multipliers[None], residual[None]


def solution(mesh):
    in_specs = (
        P("grp", "sub", None, None, None),
        P("grp", "sub", None, None),
        P("grp", "sub", None, None),
        P("grp", "sub", None, None),
        P("grp", "sub", None, None, None),
        P("grp", "sub", None),
        P("grp", "sub", None),
    )
    out_specs = (P("grp", "sub", None, None, None), P("grp", "sub", None, None, None))
    run = functools.partial(body, mesh.shape["sub"], mesh.shape["grp"])
    return jax.shard_map(run, mesh=mesh, in_specs=in_specs, out_specs=out_specs, check_vma=False)
```

```python
import functools

import jax
import jax.numpy as jnp
from jax import lax
from jax.experimental import pallas as pl
from jax.experimental.pallas import tpu as pltpu
from jax.sharding import PartitionSpec as P

FACE = 256
LOADS = 48
CDOF = 12
ITERS = 3
ORDER = 1024
PADQ = 16
TILE = 512
HALF = 64
LANES = 128
HIGHEST = lax.Precision.HIGHEST
MESH = pl.DeviceIdType.MESH
F32 = jnp.float32
BF16 = jnp.bfloat16


def dot_nn(a, b, precision=None):
    return lax.dot_general(
        a, b, (((1,), (0,)), ((), ())), precision=precision, preferred_element_type=F32
    )


def dot_nt(a, b, precision=None):
    return lax.dot_general(
        a, b, (((1,), (1,)), ((), ())), precision=precision, preferred_element_type=F32
    )


def widen(block):
    rows, columns = block.shape
    return jnp.concatenate([block, jnp.zeros((rows, LANES - columns), F32)], axis=1)


def pack_gram(gram):
    wide = widen(gram)
    half = LOADS // 2
    return wide[:half] + pltpu.roll(wide[half:], HALF, 1)


def unpack_gram(packed):
    return jnp.concatenate([packed, pltpu.roll(packed, HALF, 1)], axis=0)


def transposed(wide):
    return widen(jnp.transpose(wide)[:LOADS])


def eliminate(matrix, right):
    lane = lax.broadcasted_iota(jnp.int32, (LOADS, LANES), 1)
    row = lax.broadcasted_iota(jnp.int32, (LOADS, LANES), 0)
    symmetric = 0.5 * (matrix + transposed(matrix))
    both = jnp.where(lane < HALF, symmetric, pltpu.roll(right, HALF, 1))
    for k in range(0, LOADS, 2):
        upper, lower = both[k : k + 1, :], both[k + 1 : k + 2, :]
        first, second = both[:, k : k + 1], both[:, k + 1 : k + 2]
        inverse = 1.0 / both[k : k + 1, k : k + 1]
        beside = both[k : k + 1, k + 1 : k + 2] * inverse
        under = both[k + 1 : k + 2, k : k + 1]
        pivot = both[k + 1 : k + 2, k + 1 : k + 2] - under * beside
        upper = upper * inverse
        lower = (lower - under * upper) * (1.0 / pivot)
        rest = both - first * upper - (second - first * beside) * lower
        upper = upper - beside * lower
        both = jnp.where(row == k, upper, jnp.where(row == k + 1, lower, rest))
    return pltpu.roll(both, HALF, 1)


def kernel(
    n, ng,
    loads, inv_hbm, schur_hbm, cmap, cinv, frow, flen,
    mult_out, res_out,
    amat, qmat, tmat, pt, pcol, basis, field, from_left, from_right, from_above, from_below,
    live, resid, direc, gram_g, gram_s, term_g, part_s, part_r, cin_g, cin_t,
    load_sem, halo_ss, halo_rs, live_ss, live_rs, cin_ss, cin_rs,
    gg_ss, gg_rs, gs_ss, gs_rs, tg_ss, tg_rs, ps_ss, ps_rs,
):
    s = lax.axis_index("sub")
    g = lax.axis_index("grp")
    right, left = lax.rem(s + 1, n), lax.rem(s + n - 1, n)
    above, below = lax.rem(g + 1, ng), lax.rem(g + ng - 1, ng)

    loaded = []
    for index in range(4):
        source = (schur_hbm if index < 2 else inv_hbm).at[index % 2]
        loaded.append(pltpu.make_async_copy(source, amat.at[index], load_sem.at[index]))
        loaded[-1].start()

    barrier = pltpu.get_barrier_semaphore()
    for i in range(1, ng):
        pl.semaphore_signal(
            barrier, inc=1, device_id={"grp": lax.rem(g + i, ng)}, device_id_type=MESH
        )

    def greet(i, carry):
        pl.semaphore_signal(
            barrier, inc=1, device_id={"sub": lax.rem(s + i, n)}, device_id_type=MESH
        )
        return carry

    lax.fori_loop(1, n, greet, 0)

    position = lax.broadcasted_iota(jnp.int32, (8, FACE), 1)
    for k in range(2):
        along = (position < flen[k, 0]) & (2 * s + k < 2 * n - 1)
        around = position < flen[k, 1]
        live[1, k] = jnp.where(along, 1.0, 0.0)
        live[3, k] = jnp.where(around, 1.0, 0.0)
        field[0, 0, k] = jnp.zeros((LOADS, FACE), F32)
        field[0, 2, k] = jnp.zeros((LOADS, FACE), F32)
        field[0, 1, k] = loads[k, 0]
        field[0, 3, k] = loads[k, 1]
    live[0, 1] = live[1, 0]
    cin_g[pl.ds(g, 1)] = cinv[pl.ds(g, 1)]

    sends = []

    def send(src, dst, send_sem, recv_sem, to):
        copy = pltpu.make_async_remote_copy(
            src_ref=src, dst_ref=dst, send_sem=send_sem, recv_sem=recv_sem,
            device_id=to, device_id_type=MESH,
        )
        copy.start()
        sends.append(copy)
        return copy

    def halo_start(r, first=False):
        copies = [
            send(field.at[r, 1, 1], from_left.at[r], halo_ss.at[r, 0], halo_rs.at[r, 0], {"sub": right}),
            send(field.at[r, 3], from_below.at[r], halo_ss.at[r, 1], halo_rs.at[r, 1], {"grp": above}),
        ]
        if not first:
            copies += [
                send(field.at[r, 0, 0], from_right.at[r], halo_ss.at[r, 2], halo_rs.at[r, 2], {"sub": left}),
                send(field.at[r, 2], from_above.at[r], halo_ss.at[r, 3], halo_rs.at[r, 3], {"grp": below}),
            ]
        return copies

    def jumps(r, copies):
        for copy in copies:
            copy.wait_recv()
        first = len(copies) == 2
        pieces = []
        for k in range(2):
            for slot in range(4):
                if slot == 0:
                    other = from_left[r] if k == 0 else field[r, 1, 0]
                elif slot == 1:
                    other = field[r, 0, 1] if k == 0 else (None if first else from_right[r])
                elif slot == 2:
                    other = from_below[r, k]
                else:
                    other = None if first else from_above[r, k]
                mine = field[r, slot, k]
                jump = mine if other is None else mine - other
                pieces.append(jnp.where(live[slot, k, 0:1, :] > 0.5, jump, 0.0))
        return jnp.concatenate(pieces, axis=1)

    def store_field(r, values):
        for k in range(2):
            for slot in range(4):
                field[r, slot, k] = values[k][:, slot * FACE : (slot + 1) * FACE]

    def group_start(buffer, r, ss, rs):
        for i in range(1, ng):
            pltpu.make_async_remote_copy(
                src_ref=buffer.at[r, g], dst_ref=buffer.at[r, g],
                send_sem=ss.at[r], recv_sem=rs.at[r],
                device_id={"grp": lax.rem(g + i, ng)}, device_id_type=MESH,
            ).start()
        whole = pltpu.make_async_remote_copy(
            src_ref=buffer.at[r, pl.ds(0, ng - 1)], dst_ref=buffer.at[r, pl.ds(0, ng - 1)],
            send_sem=ss.at[r], recv_sem=rs.at[r],
            device_id={"grp": above}, device_id_type=MESH,
        )
        sends.append(whole)
        return whole

    def span_start(source, buffer, r, ss, rs, scatter):
        def step(i, carry):
            peer = lax.rem(s + i, n)
            pltpu.make_async_remote_copy(
                src_ref=source.at[r, peer if scatter else s], dst_ref=buffer.at[r, s],
                send_sem=ss.at[r], recv_sem=rs.at[r],
                device_id={"sub": peer}, device_id_type=MESH,
            ).start()
            return carry

        if n <= 8:
            for i in range(1, n):
                step(i, 0)
        else:
            lax.fori_loop(1, n, step, 0)
        whole = pltpu.make_async_remote_copy(
            src_ref=buffer.at[r, pl.ds(0, n - 1)], dst_ref=buffer.at[r, pl.ds(0, n - 1)],
            send_sem=ss.at[r], recv_sem=rs.at[r],
            device_id={"sub": right}, device_id_type=MESH,
        )
        sends.append(whole)
        return whole

    def reduce_start(r, gram):
        gram_g[r, g] = pack_gram(gram)
        return group_start(gram_g, r, gg_ss, gg_rs)

    def reduce_middle(r, whole):
        whole.wait_recv()
        gram_s[r, s] = jnp.sum(gram_g[r], axis=0)
        return span_start(gram_s, gram_s, r, gs_ss, gs_rs, False)

    def reduce_end(r, whole):
        whole.wait_recv()
        return unpack_gram(jnp.sum(gram_s[r], axis=0))

    pl.semaphore_wait(barrier, ng - 1 + n - 1)

    halo = halo_start(0, first=True)
    live_copies = [
        send(live.at[1, 1], live.at[0, 0], live_ss.at[0], live_rs.at[0], {"sub": right}),
        send(live.at[3], live.at[2], live_ss.at[1], live_rs.at[1], {"grp": above}),
    ]
    cin_copies = []
    for i in range(1, ng):
        peer = lax.rem(g + i, ng)
        cin_copies.append(
            send(cinv.at[peer], cin_g.at[g], cin_ss.at[i], cin_rs.at[i], {"grp": peer})
        )

    for k in range(2):
        rows = frow[k : k + 1, :]
        pcol[k] = jnp.transpose(jnp.broadcast_to(rows, (LANES, ORDER)))

        @pl.loop(0, ORDER // FACE)
        def _(i, k=k):
            at = pl.multiple_of(i * FACE, FACE)
            index = lax.broadcasted_iota(jnp.int32, (FACE, ORDER), 0) + at
            pt[k, pl.ds(at, FACE)] = jnp.where(index == frow[k : k + 1, :], 1.0, 0.0).astype(BF16)

    def reorder(index):
        k = index % 2
        loaded[index].wait()

        @pl.loop(0, ORDER // TILE)
        def _(i):
            at = pl.multiple_of(i * TILE, TILE)
            tmat[pl.ds(at, TILE)] = dot_nn(amat[index, pl.ds(at, TILE)], pt[k]).astype(BF16)

        @pl.loop(0, ORDER // TILE)
        def _(i):
            at = pl.multiple_of(i * TILE, TILE)
            block = pcol[k, pl.ds(at, TILE)]
            wide = jnp.concatenate([block] * (ORDER // LANES), axis=1)
            index_of = lax.broadcasted_iota(jnp.int32, (TILE, ORDER), 1)
            pick = jnp.where(index_of == wide, 1.0, 0.0).astype(BF16)
            qmat[index, pl.ds(at, TILE)] = dot_nn(pick, tmat[...]).astype(BF16)

    def apply(base, rounded):
        return [
            dot_nn(rounded[:, k * ORDER : (k + 1) * ORDER], qmat[base + k]) for k in range(2)
        ]

    reorder(0)
    reorder(1)
    for copy in live_copies:
        copy.wait_recv()
    resid[...] = jumps(0, halo)

    def precondition(r, count):
        values = apply(0, resid[...].astype(BF16))
        store_field(r, values)
        gram = dot_nt(jnp.concatenate(values, axis=1), resid[...], HIGHEST)
        stage = reduce_start(count, gram)
        return halo_start(r), stage

    halo, stage = precondition(1, 0)
    for k in range(2):
        basis[k] = dot_nn(cmap[k], pt[k]).astype(BF16)
    reorder(2)
    stage = reduce_middle(0, stage)
    for copy in cin_copies:
        copy.wait_recv()
    wide = jnp.concatenate(
        [cin_g[group, k] for k in range(2) for group in range(ng)], axis=0
    )
    cin_t[...] = jnp.transpose(wide)
    reorder(3)
    direc[...] = jumps(1, halo)
    precond_gram = reduce_end(0, stage)

    lane = lax.broadcasted_iota(jnp.int32, (LOADS, LANES), 1)
    row = lax.broadcasted_iota(jnp.int32, (LOADS, LANES), 0)
    identity = jnp.where(lane == row, 1.0, 0.0)

    r, count = 2, 1
    for iteration in range(ITERS):
        rounded = direc[...].astype(BF16)
        terms = [
            widen(dot_nt(basis[k], rounded[:, k * ORDER : (k + 1) * ORDER])) for k in range(2)
        ]
        term_g[iteration, g] = terms[0] + pltpu.roll(terms[1], HALF, 1)
        stage = group_start(term_g, iteration, tg_ss, tg_rs)
        values = apply(2, rounded)
        stage.wait_recv()
        gathered = term_g[iteration].reshape(ng * PADQ, LANES)
        stacked = jnp.concatenate([gathered, pltpu.roll(gathered, HALF, 1)], axis=0)
        shares = dot_nn(cin_t[...], stacked, HIGHEST)
        low = lax.broadcasted_iota(jnp.int32, (n * PADQ, LANES), 1) < HALF
        shares = jnp.where(low, shares[: n * PADQ], pltpu.roll(shares[n * PADQ :], HALF, 1))
        part_s[iteration] = shares.reshape(n, PADQ, LANES)
        part_r[iteration, pl.ds(s, 1)] = part_s[iteration, pl.ds(s, 1)]
        stage = span_start(part_s, part_r, iteration, ps_ss, ps_rs, True)
        stage.wait_recv()
        solved = jnp.transpose(jnp.sum(part_r[iteration], axis=0)).astype(BF16)
        values = [
            values[k] + dot_nn(solved[k * HALF : k * HALF + LOADS], basis[k]) for k in range(2)
        ]
        store_field(r, values)
        gram = dot_nt(direc[...], jnp.concatenate(values, axis=1), HIGHEST)
        stage = reduce_start(count, gram)
        halo = halo_start(r)
        stage = reduce_middle(count, stage)
        image = jumps(r, halo)
        curvature = reduce_end(count, stage)
        r, count = r + 1, count + 1
        step_size = jnp.transpose(eliminate(curvature, precond_gram))[:LOADS]
        resid[...] -= dot_nn(step_size, image, HIGHEST)
        more = iteration + 1 < ITERS
        if more:
            halo, stage = precondition(r, count)
        for k in range(2):
            for side in range(2):
                at = k * ORDER + (2 * side + 1) * FACE
                part = dot_nn(step_size, direc[:, at : at + FACE], HIGHEST)
                if iteration > 0:
                    part = mult_out[k, side] + part
                mult_out[k, side] = part
        if more:
            stage = reduce_middle(count, stage)
            inverse = eliminate(precond_gram, identity)
            search = jumps(r, halo)
            new_gram = reduce_end(count, stage)
            conjugate = dot_nn(inverse[:, :LOADS], new_gram, HIGHEST)
            weights = jnp.transpose(conjugate)[:LOADS]
            direc[...] = search + dot_nn(weights, direc[...], HIGHEST)
            precond_gram = new_gram
            r, count = r + 1, count + 1

    for k in range(2):
        for side in range(2):
            at = k * ORDER + (2 * side + 1) * FACE
            res_out[k, side] = resid[:, at : at + FACE]
    for copy in sends:
        copy.wait_send()


def body(n, ng, loads, inv_schur, schur, coarse_map, coarse_inverse, face_rows, face_len):
    basis_rows = jnp.pad(coarse_map[0], ((0, 0), (0, PADQ - CDOF), (0, 0)))
    own = coarse_inverse[0].reshape(2, CDOF, ng, n, 2, CDOF)
    own = jnp.transpose(own, (2, 0, 1, 4, 3, 5))
    pad = PADQ - CDOF
    own = jnp.pad(own, ((0, 0), (0, 0), (0, pad), (0, 0), (0, 0), (0, pad)))
    own = own.reshape(ng, 2, PADQ, 2 * n * PADQ)

    rounds, grams = 2 * ITERS + 1, 2 * ITERS
    vmem, dma = pltpu.VMEM, pltpu.SemaphoreType.DMA
    faces = jax.ShapeDtypeStruct((2, 2, LOADS, FACE), F32)
    in_vmem = pl.BlockSpec(memory_space=pltpu.VMEM)
    in_hbm = pl.BlockSpec(memory_space=pl.ANY)
    multipliers, residual = pl.pallas_call(
        functools.partial(kernel, n, ng),
        out_shape=(faces, faces),
        in_specs=[
            in_vmem, in_hbm, in_hbm, in_vmem, in_vmem, in_vmem,
            pl.BlockSpec(memory_space=pltpu.SMEM),
        ],
        out_specs=(in_vmem, in_vmem),
        scratch_shapes=[
            vmem((4, ORDER, ORDER), BF16),
            vmem((4, ORDER, ORDER), BF16),
            vmem((ORDER, ORDER), BF16),
            vmem((2, ORDER, ORDER), BF16),
            vmem((2, ORDER, LANES), jnp.int32),
            vmem((2, PADQ, ORDER), BF16),
            vmem((rounds, 4, 2, LOADS, FACE), F32),
            vmem((rounds, LOADS, FACE), F32),
            vmem((rounds, LOADS, FACE), F32),
            vmem((rounds, 2, LOADS, FACE), F32),
            vmem((rounds, 2, LOADS, FACE), F32),
            vmem((4, 2, 8, FACE), F32),
            vmem((LOADS, 2 * ORDER), F32),
            vmem((LOADS, 2 * ORDER), F32),
            vmem((grams, ng, LOADS // 2, LANES), F32),
            vmem((grams, n, LOADS // 2, LANES), F32),
            vmem((ITERS, ng, PADQ, LANES), F32),
            vmem((ITERS, n, PADQ, LANES), F32),
            vmem((ITERS, n, PADQ, LANES), F32),
            vmem((ng, 2, PADQ, 2 * n * PADQ), F32),
            vmem((2 * n * PADQ, 2 * ng * PADQ), F32),
            dma((4,)),
            dma((rounds, 4)), dma((rounds, 4)),
            dma((2,)), dma((2,)),
            dma((ng,)), dma((ng,)),
            dma((grams,)), dma((grams,)),
            dma((grams,)), dma((grams,)),
            dma((ITERS,)), dma((ITERS,)),
            dma((ITERS,)), dma((ITERS,)),
        ],
        compiler_params=pltpu.CompilerParams(
            collective_id=0, has_side_effects=True, vmem_limit_bytes=56 * 1024 * 1024
        ),
    )(loads[0], inv_schur[0], schur[0], basis_rows, own, face_rows[0], face_len[0])
    return multipliers[None], residual[None]


def solution(mesh):
    in_specs = (
        P("grp", "sub", None, None, None),
        P("grp", "sub", None, None),
        P("grp", "sub", None, None),
        P("grp", "sub", None, None),
        P("grp", "sub", None, None, None),
        P("grp", "sub", None),
        P("grp", "sub", None),
    )
    out_specs = (P("grp", "sub", None, None, None), P("grp", "sub", None, None, None))
    run = functools.partial(body, mesh.shape["sub"], mesh.shape["grp"])
    return jax.shard_map(run, mesh=mesh, in_specs=in_specs, out_specs=out_specs, check_vma=False)
```
